32 devices in a mesh: ccd: 4 (over y, core), tile: 8 (over z, x).
Axes of the slice: x: 2, y: 2, z: 4, core: 2. Of those that a mesh axis runs over, the one named last changes fastest.
Arguments:
- exposures: float32 [8, 2048, 4096], P('tile', 'ccd'), may hold values from -6 to 6
- interp: bfloat16 [8, 32, 256, 128], P('tile'), may hold values from -0.375 to 0.375
- col_offsets: int32 [8, 32], P('tile'), may hold values from 0 to 30
- template: float32 [2048, 4096], P('ccd', 'tile'), may hold values from -6 to 6
- coef_table: float32 [8, 4, 3, 3], replicated, may hold values from -3 to 3
- coef_index: int32 [8, 4, 8], replicated, may hold values from 0 to 3
- intersection: int32 [8, 4, 8], replicated, may hold values 0 or 1
Outputs:
- difference: float32 [8, 2048, 4096], P('tile', 'ccd')
The draws below stay inside these ranges and needn't reach their ends.
All inputs are finite; a program needn't handle non-finite values.
Results may differ from the reference program's by a relative error of at most 0.0029.
Values sent between devices are 32-bit elements; how exact they have to be, the bound alone decides.
A program may use at most 128 MiB of HBM per device.

```python
import jax
import jax.numpy as jnp
from jax import lax

COLS = 4096
ROWS_DEV = 512
BLOCK = 128
HALF = 10
KSETS = 4
EXPOSURES = 8
SKY_ROWS = 2048
PATCH_COLS = 512
BLOCKS = 32
PR_COUNT = 4
PC_COUNT = 8


def touch_ends(values, own_key, low, largest):
    longest = values.shape.index(max(values.shape))
    spots = []
    for shift in (0, 1):
        where = [jax.random.randint(jax.random.fold_in(own_key, axis), (), 0, length) for axis, length in enumerate(values.shape)]
        where[longest] = (where[longest] + shift) % values.shape[longest]
        spots.append(tuple(where))
    return values.at[spots[0]].set(low).at[spots[1]].set(largest)


def block_scale(rng, shape, cuts, least, high):
    gain = 1.0
    for position, parts in cuts:
        steps = jax.random.uniform(jax.random.fold_in(jax.random.fold_in(rng, 6), position), (parts,), jnp.float32, least / len(cuts), high / len(cuts))
        gain = gain * jnp.repeat(jnp.exp(steps), shape[position] // parts).reshape((-1,) + (1,) * (len(shape) - 1 - position))
    return gain


def scatter_about(key, extent, spread, most, shards=(), kind=jnp.bfloat16):
    values = spread * jax.random.normal(key, extent, jnp.float32)
    if shards:
        values = values * block_scale(key, extent, shards, -0.22, 0.18)
    return jnp.clip(values, -most, most).astype(kind)


def setup_inputs(seed: int = 0) -> dict:
    keys = jax.random.split(jax.random.key(seed), 8)
    return {
        "exposures": scatter_about(keys[0], (EXPOSURES, SKY_ROWS, COLS), 1.0, 6.0, ((0, 8), (1, 4)), jnp.float32),
        "interp": scatter_about(keys[1], (EXPOSURES, BLOCKS, 2 * BLOCK, BLOCK), (2 * BLOCK) ** -0.5, 0.375, ((0, 8),)),
        "col_offsets": touch_ends(jax.random.randint(keys[2], (EXPOSURES, BLOCKS), 0, BLOCKS - 1), jax.random.fold_in(keys[2], 1), 0, (BLOCKS - 1) - 1).astype(jnp.int32),
        "template": scatter_about(keys[3], (SKY_ROWS, COLS), 1.0, 6.0, ((0, 4), (1, 8)), jnp.float32),
        "coef_table": scatter_about(keys[4], (EXPOSURES, KSETS, 3, 3), 0.5, 3.0, (), jnp.float32),
        "coef_index": touch_ends(jax.random.randint(keys[5], (EXPOSURES, PR_COUNT, PC_COUNT), 0, KSETS), jax.random.fold_in(keys[5], 1), 0, KSETS - 1).astype(jnp.int32),
        "intersection": touch_ends((jax.random.randint(keys[6], (EXPOSURES, PR_COUNT, PC_COUNT), 0, 4) < 3).astype(jnp.int32), jax.random.fold_in(keys[6], 1), 0, 1),
    }


SIGMAS = (1.5, 3.0, 5.0)


def basis_taps(half_width):
    positions = jnp.arange(-half_width, half_width + 1).astype(jnp.float32)
    kernels = []
    for sigma_value in SIGMAS:
        gauss = jnp.exp(-0.5 * (positions / sigma_value) ** 2)
        kernels.append(gauss / jnp.sum(gauss))
    return kernels


def smooth(padded, gauss, out_rows, out_cols):
    tap_count = gauss.shape[0]
    across = gauss[0] * padded[0:out_rows, :]
    for offset in range(1, tap_count):
        across = across + gauss[offset] * padded[offset:offset + out_rows, :]
    result = gauss[0] * across[:, 0:out_cols]
    for offset in range(1, tap_count):
        result = result + gauss[offset] * across[:, offset:offset + out_cols]
    return result


def resample(exposure_img, weights, offsets):
    row_count = exposure_img.shape[0]
    tiles = exposure_img.astype(jnp.bfloat16).reshape(row_count, BLOCKS, BLOCK)
    first_part = jnp.take(tiles, offsets, axis=1)
    second_part = jnp.take(tiles, offsets + 1, axis=1)
    window = jnp.concatenate([first_part, second_part], axis=2)
    output = jnp.einsum("rjk,jkn->rjn", window.astype(jnp.float32), weights.astype(jnp.float32))
    return output.reshape(row_count, BLOCKS * BLOCK)


def expand(grid):
    return jnp.repeat(jnp.repeat(grid, ROWS_DEV, axis=0), PATCH_COLS, axis=1)


def reference(exposures, interp, col_offsets, template, coef_table, coef_index, intersection):
    kernels = basis_taps(HALF)
    padded = jnp.pad(template, HALF)
    smoothed = [smooth(padded, gauss, SKY_ROWS, COLS) for gauss in kernels]
    row_coord = ((jnp.arange(SKY_ROWS) % ROWS_DEV).astype(jnp.float32) - (ROWS_DEV - 1) / 2.0) / (ROWS_DEV / 2.0)
    col_coord = ((jnp.arange(COLS) % PATCH_COLS).astype(jnp.float32) - (PATCH_COLS - 1) / 2.0) / (PATCH_COLS / 2.0)

    def visit(operands):
        exposure_img, weights, offsets, table, indices, covered = operands
        warped = resample(exposure_img, weights, offsets)
        set_pick = (indices[:, :, None] == jnp.arange(KSETS)[None, None, :]).astype(jnp.float32)
        kernel_coef = jnp.sum(set_pick[:, :, :, None, None] * table[None, None], axis=2)
        template_model = None
        for kernel_index in range(3):
            pieces = [expand(kernel_coef[:, :, kernel_index, component]) for component in range(3)]
            weight_map = (pieces[0] + pieces[1] * col_coord[None, :]) + pieces[2] * row_coord[:, None]
            contrib = weight_map * smoothed[kernel_index]
            template_model = contrib if template_model is None else template_model + contrib
        coverage = expand(covered.astype(jnp.float32))
        return (warped - template_model) * coverage

    return lax.map(visit, (exposures, interp, col_offsets, coef_table, coef_index, intersection))
```

```python
import functools

import jax
import jax.numpy as jnp
import ml_dtypes
import numpy as np
from jax import lax
from jax.experimental import pallas as pl
from jax.experimental.pallas import tpu as pltpu
from jax.sharding import PartitionSpec as P

HALF = 10
KSETS = 4
SIGMAS = (1.5, 3.0, 5.0)
HALO = 16
EDGE = 128
BAND = 128
CHUNKS = 2
LINES = 128


def basis_taps():
    positions = np.arange(-HALF, HALF + 1).astype(np.float64)
    kernels = []
    for sigma_value in SIGMAS:
        gauss = np.exp(-0.5 * (positions / sigma_value) ** 2)
        kernels.append(gauss / np.sum(gauss))
    return kernels


def banded(taps, rows, cols, shift):
    distance = np.arange(cols)[None, :] - np.arange(rows)[:, None] - shift
    inside = np.abs(distance) <= HALF
    return np.where(inside, taps[np.clip(distance + HALF, 0, 2 * HALF)], 0.0)


def smoothing_matrices(patch_cols):
    down, across, gains = [], [], []
    for taps in basis_taps():
        near = taps.astype(ml_dtypes.bfloat16)
        down.append(banded(taps, BAND, BAND + 2 * HALO, HALO))
        across.append(banded(taps, patch_cols, patch_cols + 2 * EDGE, EDGE))
        gains.append(1.0 / np.sum(near.astype(np.float64)) ** 2)
    as_bf16 = lambda parts: np.stack(parts).astype(ml_dtypes.bfloat16)
    return np.concatenate(list(as_bf16(down)), axis=0), as_bf16(across), gains


def inner_size(count):
    best = 1
    for size in range(1, count + 1):
        if count % size == 0 and size * size <= count:
            best = size
    return best


def arrival_codes(count):
    inner = inner_size(count)
    codes = []
    for me in range(count):
        z, x = divmod(me, inner)
        near = sorted(range(count // inner), key=lambda other: (abs(other - z), other))
        keys = []
        for q in range(count):
            if q == me:
                continue
            qz, qx = divmod(q, inner)
            away = abs(qz - z)
            time = away if qx == x else max(near.index(qz), away) + abs(qx - x)
            keys.append((time, qx != x, q))
        order = [q for _, _, q in sorted(keys)]
        words = []
        for first in range(0, count - 1, 7):
            words.append(sum(q << (4 * i) for i, q in enumerate(order[first : first + 7])))
        codes.append(words)
    return codes


def model_kernel(
    count, ccd_count, template, weights, down, across, out,
    strip, load_sem, send_sem, recv_sem, hsend_sem, hrecv_sem,
):
    me = lax.axis_index("tile")
    row = lax.axis_index("ccd")
    inner = inner_size(count)
    outer = count // inner
    z, x = me // inner, me % inner
    rows, patch_cols = template.shape
    cols = out.shape[1]
    part = rows // CHUNKS

    targets = (me - inner, me + inner, me - 1, me + 1)
    there = (z > 0, z < outer - 1, x > 0, x < inner - 1)
    halo_there = (row > 0, row < ccd_count - 1)

    load = pltpu.make_async_copy(template, strip.at[me, pl.ds(HALO, rows)], load_sem)
    load.start()

    barrier = pltpu.get_barrier_semaphore()
    total = jnp.int32(0)
    for target, exists in zip(targets, there):
        @pl.when(exists)
        def _():
            pl.semaphore_signal(barrier, inc=1, device_id=(row, target))
        total = total + exists.astype(jnp.int32)
    for step, exists in zip((-1, 1), halo_there):
        @pl.when(exists)
        def _():
            pl.semaphore_signal(barrier, inc=1, device_id=(row + step, me))
        total = total + exists.astype(jnp.int32)
    pl.semaphore_wait(barrier, total)

    def send(q, c, d, own):
        piece = pl.ds(HALO + c * part, part)
        return pltpu.make_async_remote_copy(
            src_ref=template.at[pl.ds(c * part, part)] if own else strip.at[q, piece],
            dst_ref=strip.at[q, piece],
            send_sem=send_sem.at[d, q, c],
            recv_sem=recv_sem.at[q, c],
            device_id=(row, targets[d]),
        )

    def halo(q, d):
        source = pl.ds(HALO, HALO) if d == 0 else pl.ds(rows, HALO)
        target = pl.ds(HALO + rows, HALO) if d == 0 else pl.ds(0, HALO)
        return pltpu.make_async_remote_copy(
            src_ref=strip.at[q, source],
            dst_ref=strip.at[q, target],
            send_sem=hsend_sem.at[d, q],
            recv_sem=hrecv_sem.at[d, q],
            device_id=(row + (-1 if d == 0 else 1), me),
        )

    def routes(q):
        qz, qx = q // inner, q % inner
        same = qx == x
        return (
            same & (qz > z) & there[0],
            same & (qz < z) & there[1],
            ((qx > x) | same) & there[2],
            ((qx < x) | same) & there[3],
        )

    for c in range(CHUNKS):
        for d in range(4):
            @pl.when(there[d])
            def _():
                send(me, c, d, True).start()
    load.wait()
    for d in range(2):
        @pl.when(halo_there[d])
        def _():
            halo(me, d).start()

    @pl.when(row == 0)
    def _():
        for q in range(count):
            strip[q, 0:HALO, :] = jnp.zeros((HALO, patch_cols), jnp.float32)

    @pl.when(row == ccd_count - 1)
    def _():
        for q in range(count):
            strip[q, rows + HALO : rows + 2 * HALO, :] = jnp.zeros((HALO, patch_cols), jnp.float32)

    out[...] = jnp.zeros_like(out)

    def add_model(q):
        first = pl.multiple_of(q * patch_cols, EDGE)
        wide = patch_cols + 2 * EDGE
        left = pl.multiple_of(jnp.maximum(first - EDGE, 0), EDGE)
        right = pl.multiple_of(jnp.minimum(first + patch_cols, cols - EDGE), EDGE)

        def band(r, carry):
            at = pl.multiple_of(r * BAND, BAND)
            lines = pl.ds(at, BAND)
            pixel = strip[q, pl.ds(at, BAND + 2 * HALO), :].astype(jnp.bfloat16)
            tall = jnp.dot(down[...], pixel, preferred_element_type=jnp.float32)
            tall = tall.astype(jnp.bfloat16)
            v = (
                lax.broadcasted_iota(jnp.int32, (BAND, wide), 0) + r * BAND
            ).astype(jnp.float32) * (2.0 / rows) - (rows - 1) / rows
            model = None
            for b in range(3):
                flat = jnp.dot(
                    tall[b * BAND : (b + 1) * BAND], across[b], preferred_element_type=jnp.float32
                )
                const = weights[b : b + 1, pl.ds(first, wide)]
                slope = weights[3 + b : 4 + b, pl.ds(first, wide)]
                term = (const + slope * v) * flat
                model = term if model is None else model + term
            out[lines, pl.ds(first, patch_cols)] += model[:, EDGE : EDGE + patch_cols]
            out[lines, pl.ds(left, EDGE)] += model[:, :EDGE]
            out[lines, pl.ds(right, EDGE)] += model[:, EDGE + patch_cols :]
            return carry

        lax.fori_loop(0, rows // BAND, band, 0)

    def halos_in(q):
        for d in range(2):
            @pl.when(halo_there[1 - d])
            def _():
                halo(q, d).wait_recv()

    halos_in(me)
    add_model(me)

    table = arrival_codes(count)
    words = []
    for w in range(len(table[0])):
        word = jnp.int32(0)
        for i in range(count):
            word = jnp.where(me == i, jnp.int32(table[i][w]), word)
        words.append(word)

    def arrive(_, words):
        words = list(words)
        q = words[0] % 16
        for w in range(len(words)):
            words[w] = words[w] // 16
            if w + 1 < len(words):
                words[w] = words[w] + (words[w + 1] % 16) * (1 << 24)
        onward = routes(q)
        for c in range(CHUNKS):
            send(q, c, 0, False).wait_recv()
            for d in range(4):
                @pl.when(onward[d])
                def _():
                    send(q, c, d, False).start()
        for d in range(2):
            @pl.when(halo_there[d])
            def _():
                halo(q, d).start()
        halos_in(q)
        add_model(q)
        return tuple(words)

    lax.fori_loop(0, count - 1, arrive, tuple(words))

    def drain(q, carry):
        onward = routes(q)
        for d in range(4):
            @pl.when(jnp.where(q == me, there[d], onward[d]))
            def _():
                for c in range(CHUNKS):
                    send(q, c, d, False).wait_send()
        for d in range(2):
            @pl.when(halo_there[d])
            def _():
                halo(q, d).wait_send()
        return carry

    lax.fori_loop(0, count, drain, 0)


def difference_kernel(offsets, exposure, mats, model, weights, out, pixels):
    blocks, depth, block = mats.shape
    pixels[...] = exposure[...].astype(jnp.bfloat16)
    for j in range(blocks):
        start = pl.multiple_of(offsets[j] * block, block)
        value = jnp.dot(
            pixels[:, pl.ds(start, depth)], mats[j], preferred_element_type=jnp.float32
        )
        here = slice(j * block, (j + 1) * block)
        covered = weights[6:7, EDGE + j * block : EDGE + (j + 1) * block]
        out[:, here] = value * covered - model[:, here]


def on_device(exposures, interp, col_offsets, template, coef_table, coef_index, intersection):
    rows, cols = exposures.shape[1:]
    patch_cols = template.shape[1]
    count, ccd_count = lax.axis_size("tile"), lax.axis_size("ccd")
    patch_row = lax.axis_index("ccd")
    my_epoch = lax.axis_index("tile")
    down, across, gains = smoothing_matrices(patch_cols)

    set_ids = coef_index[my_epoch, patch_row]
    set_pick = (set_ids[:, None] == jnp.arange(KSETS)[None, :]).astype(jnp.float32)
    coef = jnp.sum(set_pick[:, :, None, None] * coef_table[my_epoch][None], axis=1)
    covered = intersection[my_epoch, patch_row].astype(jnp.float32)
    coef = coef * covered[:, None, None] * jnp.asarray(gains, jnp.float32)[None, :, None]
    u = (jnp.arange(patch_cols).astype(jnp.float32) - (patch_cols - 1) / 2.0) / (patch_cols / 2.0)
    spread = coef.transpose(1, 2, 0)[:, :, :, None]
    const = (spread[:, 0] + spread[:, 1] * u[None, None, :]).reshape(3, cols)
    slope = jnp.broadcast_to(spread[:, 2], (3, count, patch_cols)).reshape(3, cols)
    cover = jnp.broadcast_to(covered[None, :, None], (2, count, patch_cols)).reshape(2, cols)
    weights = jnp.pad(jnp.concatenate([const, slope, cover]), ((0, 0), (EDGE, EDGE)))

    anywhere = pl.BlockSpec(memory_space=pl.ANY)
    vmem = pl.BlockSpec(memory_space=pltpu.VMEM)
    model = pl.pallas_call(
        functools.partial(model_kernel, count, ccd_count),
        out_shape=jax.ShapeDtypeStruct((rows, cols), jnp.float32),
        in_specs=[anywhere, vmem, vmem, vmem],
        out_specs=vmem,
        scratch_shapes=[
            pltpu.VMEM((count, rows + 2 * HALO, patch_cols), jnp.float32),
            pltpu.SemaphoreType.DMA,
            pltpu.SemaphoreType.DMA((4, count, CHUNKS)),
            pltpu.SemaphoreType.DMA((count, CHUNKS)),
            pltpu.SemaphoreType.DMA((2, count)),
            pltpu.SemaphoreType.DMA((2, count)),
        ],
        compiler_params=pltpu.CompilerParams(
            collective_id=0, has_side_effects=True, vmem_limit_bytes=32 * 2**20
        ),
    )(template, weights, down, across)

    blocks, depth, block = interp.shape[1:]
    lines = min(LINES, rows)
    result = pl.pallas_call(
        difference_kernel,
        grid=(rows // lines,),
        out_shape=jax.ShapeDtypeStruct((rows, cols), jnp.float32),
        in_specs=[
            pl.BlockSpec(memory_space=pltpu.SMEM),
            pl.BlockSpec((lines, cols), lambda i: (i, 0)),
            pl.BlockSpec((blocks, depth, block), lambda i: (0, 0, 0)),
            pl.BlockSpec((lines, cols), lambda i: (i, 0)),
            pl.BlockSpec(weights.shape, lambda i: (0, 0)),
        ],
        out_specs=pl.BlockSpec((lines, cols), lambda i: (i, 0)),
        scratch_shapes=[pltpu.VMEM((lines, cols), jnp.bfloat16)],
        compiler_params=pltpu.CompilerParams(vmem_limit_bytes=32 * 2**20),
    )(col_offsets[0], exposures[0], interp[0], model, weights)
    return result[None]


def solution(mesh):
    placed = (
        P("tile", "ccd", None),
        P("tile", None, None, None),
        P("tile", None),
        P("ccd", "tile"),
        P(),
        P(),
        P(),
    )
    return jax.shard_map(
        on_device, mesh=mesh, in_specs=placed, out_specs=P("tile", "ccd", None), check_vma=False
    )
```

```python
import functools
import heapq

import jax
import jax.numpy as jnp
import ml_dtypes
import numpy as np
from jax import lax
from jax.experimental import pallas as pl
from jax.experimental.pallas import tpu as pltpu
from jax.sharding import PartitionSpec as P

HALF = 10
KSETS = 4
SIGMAS = (1.5, 3.0, 5.0)
HALO = 16
EDGE = 128
BAND = 128
CHUNKS = 4
LINES = 128


def basis_taps():
    positions = np.arange(-HALF, HALF + 1).astype(np.float64)
    kernels = []
    for sigma_value in SIGMAS:
        gauss = np.exp(-0.5 * (positions / sigma_value) ** 2)
        kernels.append(gauss / np.sum(gauss))
    return kernels


def smoothing_gains():
    near = [taps.astype(ml_dtypes.bfloat16).astype(np.float64) for taps in basis_taps()]
    return [1.0 / np.sum(taps) ** 2 for taps in near]


def banded(b, rows, cols, shift, first=0):
    shape = (rows, cols)
    distance = (
        lax.broadcasted_iota(jnp.int32, shape, 1)
        - lax.broadcasted_iota(jnp.int32, shape, 0)
        - (shift + first)
    )
    away = distance.astype(jnp.float32)
    taps = jnp.exp(away * away * (-0.5 / SIGMAS[b] ** 2)) * basis_taps()[b][HALF]
    return jnp.where(jnp.abs(away) <= HALF, taps, 0.0).astype(jnp.bfloat16)


def inner_size(count):
    best = 1
    for size in range(1, count + 1):
        if count % size == 0 and size * size <= count:
            best = size
    return best


def routes(outer, inner, me, q, c):
    z, x = divmod(me, inner)
    qz, qx = divmod(q, inner)
    detour = inner == 2 and outer > 2 and c >= CHUNKS // 2 and qz in (0, outer - 1)
    along = qx == x or detour
    return (
        along and qz >= z > 0,
        along and qz <= z < outer - 1,
        (q == me or (not detour and qx >= x)) and x > 0,
        (q == me or (not detour and qx <= x)) and x < inner - 1,
    )


def arrival_events(count):
    inner = inner_size(count)
    outer = count // inner
    steps = (-inner, inner, -1, 1)
    queue, free, tick = [], {}, 0
    seen = [[] for _ in range(count)]
    for q in range(count):
        for d in range(4):
            for c in range(CHUNKS) if d < 2 else reversed(range(CHUNKS)):
                if routes(outer, inner, q, q, c)[d]:
                    heapq.heappush(queue, (0, tick, q, d, q, c))
                    tick += 1
    while queue:
        ready, _, me, d, q, c = heapq.heappop(queue)
        if ready < free.get((me, d), 0):
            heapq.heappush(queue, (free[me, d], tick, me, d, q, c))
            tick += 1
            continue
        free[me, d] = ready + 1
        there = me + steps[d]
        seen[there].append((ready + 1, tick, q * CHUNKS + c))
        for onward in range(4):
            if routes(outer, inner, there, q, c)[onward]:
                heapq.heappush(queue, (ready + 1, tick, there, onward, q, c))
                tick += 1
    return [[event for _, _, event in sorted(arrivals)] for arrivals in seen]


DIGIT = 256
PER_WORD = 3


def arrival_codes(count):
    codes = []
    for events in arrival_events(count):
        assert len(events) == (count - 1) * CHUNKS
        left = {q: CHUNKS for q in range(count)}
        digits = []
        for event in events:
            left[event // CHUNKS] -= 1
            digits.append(event * 2 + (left[event // CHUNKS] == 0))
        codes.append([
            sum(int(v) * DIGIT**i for i, v in enumerate(digits[first : first + PER_WORD]))
            for first in range(0, len(digits), PER_WORD)
        ])
    return codes


def model_kernel(
    count, ccd_count, template, weights, out,
    strip, down, across, load_sem, send_sem, recv_sem, hsend_sem, hrecv_sem,
):
    me = lax.axis_index("tile")
    row = lax.axis_index("ccd")
    inner = inner_size(count)
    outer = count // inner
    z, x = me // inner, me % inner
    rows, patch_cols = template.shape
    cols = out.shape[1]
    part = rows // CHUNKS

    targets = (me - inner, me + inner, me - 1, me + 1)
    there = (z > 0, z < outer - 1, x > 0, x < inner - 1)
    halo_there = (row > 0, row < ccd_count - 1)

    load = pltpu.make_async_copy(template, strip.at[me, pl.ds(HALO, rows)], load_sem)
    load.start()

    barrier = pltpu.get_barrier_semaphore()
    total = jnp.int32(0)
    for target, exists in zip(targets, there):
        @pl.when(exists)
        def _():
            pl.semaphore_signal(barrier, inc=1, device_id=(row, target))
        total = total + exists.astype(jnp.int32)
    for step, exists in zip((-1, 1), halo_there):
        @pl.when(exists)
        def _():
            pl.semaphore_signal(barrier, inc=1, device_id=(row + step, me))
        total = total + exists.astype(jnp.int32)
    pl.semaphore_wait(barrier, total)

    def send(q, c, d, own):
        piece = pl.ds(pl.multiple_of(HALO + c * part, HALO), part)
        return pltpu.make_async_remote_copy(
            src_ref=template.at[pl.ds(c * part, part)] if own else strip.at[q, piece],
            dst_ref=strip.at[q, piece],
            send_sem=send_sem.at[d, q, c],
            recv_sem=recv_sem.at[q, c],
            device_id=(row, targets[d]),
        )

    def halo(q, d):
        source = pl.ds(HALO, HALO) if d == 0 else pl.ds(rows, HALO)
        target = pl.ds(HALO + rows, HALO) if d == 0 else pl.ds(0, HALO)
        return pltpu.make_async_remote_copy(
            src_ref=strip.at[q, source],
            dst_ref=strip.at[q, target],
            send_sem=hsend_sem.at[d, q],
            recv_sem=hrecv_sem.at[d, q],
            device_id=(row + (-1 if d == 0 else 1), me),
        )

    for d in (0, 2, 1, 3):
        for c in range(CHUNKS) if d < 2 else reversed(range(CHUNKS)):
            @pl.when(there[d])
            def _():
                send(me, c, d, True).start()
    load.wait()
    for d in range(2):
        @pl.when(halo_there[d])
        def _():
            halo(me, d).start()

    @pl.when(row == 0)
    def _():
        for q in range(count):
            strip[q, 0:HALO, :] = jnp.zeros((HALO, patch_cols), jnp.float32)

    @pl.when(row == ccd_count - 1)
    def _():
        for q in range(count):
            strip[q, rows + HALO : rows + 2 * HALO, :] = jnp.zeros((HALO, patch_cols), jnp.float32)

    def clear(r, carry):
        out[pl.ds(pl.multiple_of(r * HALO, HALO), HALO), :] = jnp.zeros((HALO, cols), jnp.float32)
        return carry

    lax.fori_loop(0, rows // HALO, clear, 0)

    def add_model(q):
        first = pl.multiple_of(q * patch_cols, EDGE)
        wide = patch_cols + 2 * EDGE
        left = pl.multiple_of(jnp.maximum(first - EDGE, 0), EDGE)
        right = pl.multiple_of(jnp.minimum(first + patch_cols, cols - EDGE), EDGE)

        def band(r, carry):
            at = pl.multiple_of(r * BAND, BAND)
            lines = pl.ds(at, BAND)
            pixel = strip[q, pl.ds(at, BAND + 2 * HALO), :].astype(jnp.bfloat16)
            tall = jnp.dot(down[...], pixel, preferred_element_type=jnp.float32)
            tall = tall.astype(jnp.bfloat16)
            v = (
                lax.broadcasted_iota(jnp.int32, (BAND, wide), 0) + r * BAND
            ).astype(jnp.float32) * (2.0 / rows) - (rows - 1) / rows
            model = None
            for b in range(3):
                flat = jnp.dot(
                    tall[b * BAND : (b + 1) * BAND], across[b], preferred_element_type=jnp.float32
                )
                const = weights[b : b + 1, pl.ds(first, wide)]
                slope = weights[3 + b : 4 + b, pl.ds(first, wide)]
                term = (const + slope * v) * flat
                model = term if model is None else model + term
            out[lines, pl.ds(first, patch_cols)] += model[:, EDGE : EDGE + patch_cols]
            out[lines, pl.ds(left, EDGE)] += model[:, :EDGE]
            out[lines, pl.ds(right, EDGE)] += model[:, EDGE + patch_cols :]
            return carry

        lax.fori_loop(0, rows // BAND, band, 0)

    def halos_in(q):
        for d in range(2):
            @pl.when(halo_there[1 - d])
            def _():
                halo(q, d).wait_recv()

    for b in range(3):
        down[b * BAND : (b + 1) * BAND, :] = banded(b, BAND, BAND + 2 * HALO, HALO)

        def fill(i, carry):
            first = pl.multiple_of(i * HALO, HALO)
            across[b, pl.ds(first, HALO), :] = banded(
                b, HALO, patch_cols + 2 * EDGE, EDGE, i * HALO
            )
            return carry

        lax.fori_loop(0, patch_cols // HALO, fill, 0)

    halos_in(me)
    add_model(me)

    def paths(q, c):
        qz, qx = q // inner, q % inner
        detour = jnp.zeros((), jnp.bool_)
        if inner == 2 and outer > 2:
            detour = (c >= CHUNKS // 2) & ((qz == 0) | (qz == outer - 1))
        own = q == me
        along = (qx == x) | detour
        level = jnp.logical_not(detour)
        return (
            along & (qz >= z) & there[0],
            along & (qz <= z) & there[1],
            (own | level & (qx >= x)) & there[2],
            (own | level & (qx <= x)) & there[3],
        )

    table = arrival_codes(count)
    words = []
    for w in range(len(table[0])):
        word = jnp.int32(0)
        for i in range(count):
            word = jnp.where(me == i, jnp.int32(table[i][w]), word)
        words.append(word)

    def arrive(_, words):
        words = list(words)
        digit = words[0] % DIGIT
        for w in range(len(words)):
            words[w] = words[w] // DIGIT
            if w + 1 < len(words):
                words[w] = words[w] + (words[w + 1] % DIGIT) * DIGIT ** (PER_WORD - 1)
        done, event = digit % 2, digit // 2
        q, c = event // CHUNKS, event % CHUNKS
        send(q, c, 0, False).wait_recv()
        onward = paths(q, c)
        for d in range(4):
            @pl.when(onward[d])
            def _():
                send(q, c, d, False).start()
        for d in range(2):
            @pl.when((c == (0 if d == 0 else CHUNKS - 1)) & halo_there[d])
            def _():
                halo(q, d).start()

        @pl.when(done == 1)
        def _():
            halos_in(q)
            add_model(q)

        return tuple(words)

    lax.fori_loop(0, (count - 1) * CHUNKS, arrive, tuple(words))

    def drain(event, carry):
        q, c = event // CHUNKS, event % CHUNKS
        onward = paths(q, c)
        for d in range(4):
            @pl.when(onward[d])
            def _():
                send(q, c, d, False).wait_send()
        for d in range(2):
            @pl.when((c == 0) & halo_there[d])
            def _():
                halo(q, d).wait_send()
        return carry

    lax.fori_loop(0, count * CHUNKS, drain, 0)


def difference_kernel(offsets, exposure, mats, model, weights, out, pixels):
    blocks, depth, block = mats.shape
    pixels[...] = exposure[...].astype(jnp.bfloat16)
    for j in range(blocks):
        start = pl.multiple_of(offsets[j] * block, block)
        value = jnp.dot(
            pixels[:, pl.ds(start, depth)], mats[j], preferred_element_type=jnp.float32
        )
        here = slice(j * block, (j + 1) * block)
        covered = weights[6:7, EDGE + j * block : EDGE + (j + 1) * block]
        out[:, here] = value * covered - model[:, here]


def on_device(exposures, interp, col_offsets, template, coef_table, coef_index, intersection):
    rows, cols = exposures.shape[1:]
    patch_cols = template.shape[1]
    count, ccd_count = lax.axis_size("tile"), lax.axis_size("ccd")
    patch_row = lax.axis_index("ccd")
    my_epoch = lax.axis_index("tile")
    gains = smoothing_gains()

    set_ids = coef_index[my_epoch, patch_row]
    set_pick = (set_ids[:, None] == jnp.arange(KSETS)[None, :]).astype(jnp.float32)
    coef = jnp.sum(set_pick[:, :, None, None] * coef_table[my_epoch][None], axis=1)
    covered = intersection[my_epoch, patch_row].astype(jnp.float32)
    coef = coef * covered[:, None, None] * jnp.asarray(gains, jnp.float32)[None, :, None]
    u = (jnp.arange(patch_cols).astype(jnp.float32) - (patch_cols - 1) / 2.0) / (patch_cols / 2.0)
    spread = coef.transpose(1, 2, 0)[:, :, :, None]
    const = (spread[:, 0] + spread[:, 1] * u[None, None, :]).reshape(3, cols)
    slope = jnp.broadcast_to(spread[:, 2], (3, count, patch_cols)).reshape(3, cols)
    cover = jnp.broadcast_to(covered[None, :, None], (2, count, patch_cols)).reshape(2, cols)
    weights = jnp.pad(jnp.concatenate([const, slope, cover]), ((0, 0), (EDGE, EDGE)))

    in_hbm = pl.BlockSpec(memory_space=pltpu.HBM)
    vmem = pl.BlockSpec(memory_space=pltpu.VMEM)
    model = pl.pallas_call(
        functools.partial(model_kernel, count, ccd_count),
        out_shape=jax.ShapeDtypeStruct((rows, cols), jnp.float32),
        in_specs=[in_hbm, vmem],
        out_specs=vmem,
        scratch_shapes=[
            pltpu.VMEM((count, rows + 2 * HALO, patch_cols), jnp.float32),
            pltpu.VMEM((3 * BAND, BAND + 2 * HALO), jnp.bfloat16),
            pltpu.VMEM((3, patch_cols, patch_cols + 2 * EDGE), jnp.bfloat16),
            pltpu.SemaphoreType.DMA,
            pltpu.SemaphoreType.DMA((4, count, CHUNKS)),
            pltpu.SemaphoreType.DMA((count, CHUNKS)),
            pltpu.SemaphoreType.DMA((2, count)),
            pltpu.SemaphoreType.DMA((2, count)),
        ],
        compiler_params=pltpu.CompilerParams(
            collective_id=0, has_side_effects=True, vmem_limit_bytes=32 * 2**20
        ),
    )(template, weights)

    blocks, depth, block = interp.shape[1:]
    lines = min(LINES, rows)
    result = pl.pallas_call(
        difference_kernel,
        grid=(rows // lines,),
        out_shape=jax.ShapeDtypeStruct((rows, cols), jnp.float32),
        in_specs=[
            pl.BlockSpec(memory_space=pltpu.SMEM),
            pl.BlockSpec((lines, cols), lambda i: (i, 0)),
            pl.BlockSpec((blocks, depth, block), lambda i: (0, 0, 0)),
            pl.BlockSpec((lines, cols), lambda i: (i, 0)),
            pl.BlockSpec(weights.shape, lambda i: (0, 0)),
        ],
        out_specs=pl.BlockSpec((lines, cols), lambda i: (i, 0)),
        scratch_shapes=[pltpu.VMEM((lines, cols), jnp.bfloat16)],
        compiler_params=pltpu.CompilerParams(vmem_limit_bytes=32 * 2**20),
    )(col_offsets[0], exposures[0], interp[0], model, weights)
    return result[None]


def solution(mesh):
    placed = (
        P("tile", "ccd", None),
        P("tile", None, None, None),
        P("tile", None),
        P("ccd", "tile"),
        P(),
        P(),
        P(),
    )
    return jax.shard_map(
        on_device, mesh=mesh, in_specs=placed, out_specs=P("tile", "ccd", None), check_vma=False
    )
```

```python
import functools

import jax
import jax.numpy as jnp
import ml_dtypes
import numpy as np
from jax import lax
from jax.experimental import pallas as pl
from jax.experimental.pallas import tpu as pltpu
from jax.sharding import PartitionSpec as P

HALF = 10
KSETS = 4
SIGMAS = (1.5, 3.0, 5.0)
HALO = 16
EDGE = 128
BAND = 128
CHUNKS = 2
LINES = 128


def basis_taps():
    positions = np.arange(-HALF, HALF + 1).astype(np.float64)
    kernels = []
    for sigma_value in SIGMAS:
        gauss = np.exp(-0.5 * (positions / sigma_value) ** 2)
        kernels.append(gauss / np.sum(gauss))
    return kernels


def smoothing_gains():
    near = [taps.astype(ml_dtypes.bfloat16).astype(np.float64) for taps in basis_taps()]
    return [1.0 / np.sum(taps) ** 2 for taps in near]


def banded(b, rows, cols, shift, first=0):
    shape = (rows, cols)
    distance = (
        lax.broadcasted_iota(jnp.int32, shape, 1)
        - lax.broadcasted_iota(jnp.int32, shape, 0)
        - (shift + first)
    )
    away = distance.astype(jnp.float32)
    taps = jnp.exp(away * away * (-0.5 / SIGMAS[b] ** 2)) * basis_taps()[b][HALF]
    return jnp.where(jnp.abs(away) <= HALF, taps, 0.0).astype(jnp.bfloat16)


def inner_size(count):
    best = 1
    for size in range(1, count + 1):
        if count % size == 0 and size * size <= count:
            best = size
    return best


def arrival_events(count):
    inner = inner_size(count)
    events = []
    for me in range(count):
        z, x = divmod(me, inner)
        near = sorted(range(count // inner), key=lambda other: (abs(other - z), other))
        keys = []
        for q in range(count):
            if q == me:
                continue
            qz, qx = divmod(q, inner)
            away = abs(qz - z)
            time = away if qx == x else max(near.index(qz), away) + abs(qx - x)
            keys.append((time, qx != x, q))
        events.append([q * CHUNKS + c for _, _, q in sorted(keys) for c in range(CHUNKS)])
    return events


DIGIT = 256
PER_WORD = 3


def arrival_codes(count):
    codes = []
    for events in arrival_events(count):
        assert len(events) == (count - 1) * CHUNKS
        left = {q: CHUNKS for q in range(count)}
        digits = []
        for event in events:
            left[event // CHUNKS] -= 1
            digits.append(event * 2 + (left[event // CHUNKS] == 0))
        codes.append([
            sum(int(v) * DIGIT**i for i, v in enumerate(digits[first : first + PER_WORD]))
            for first in range(0, len(digits), PER_WORD)
        ])
    return codes


def model_kernel(
    count, ccd_count, template, weights, out,
    strip, down, across, load_sem, send_sem, recv_sem, hsend_sem, hrecv_sem,
):
    me = lax.axis_index("tile")
    row = lax.axis_index("ccd")
    inner = inner_size(count)
    outer = count // inner
    z, x = me // inner, me % inner
    rows, patch_cols = template.shape
    cols = out.shape[1]
    part = rows // CHUNKS

    targets = (me - inner, me + inner, me - 1, me + 1)
    there = (z > 0, z < outer - 1, x > 0, x < inner - 1)
    halo_there = (row > 0, row < ccd_count - 1)

    load = pltpu.make_async_copy(template, strip.at[me, pl.ds(HALO, rows)], load_sem)
    load.start()

    barrier = pltpu.get_barrier_semaphore()
    total = jnp.int32(0)
    for target, exists in zip(targets, there):
        @pl.when(exists)
        def _():
            pl.semaphore_signal(barrier, inc=1, device_id=(row, target))
        total = total + exists.astype(jnp.int32)
    for step, exists in zip((-1, 1), halo_there):
        @pl.when(exists)
        def _():
            pl.semaphore_signal(barrier, inc=1, device_id=(row + step, me))
        total = total + exists.astype(jnp.int32)
    pl.semaphore_wait(barrier, total)

    def send(q, c, d, own):
        piece = pl.ds(pl.multiple_of(HALO + c * part, HALO), part)
        return pltpu.make_async_remote_copy(
            src_ref=template.at[pl.ds(c * part, part)] if own else strip.at[q, piece],
            dst_ref=strip.at[q, piece],
            send_sem=send_sem.at[d, q, c],
            recv_sem=recv_sem.at[q, c],
            device_id=(row, targets[d]),
        )

    def halo(q, d):
        source = pl.ds(HALO, HALO) if d == 0 else pl.ds(rows, HALO)
        target = pl.ds(HALO + rows, HALO) if d == 0 else pl.ds(0, HALO)
        return pltpu.make_async_remote_copy(
            src_ref=strip.at[q, source],
            dst_ref=strip.at[q, target],
            send_sem=hsend_sem.at[d, q],
            recv_sem=hrecv_sem.at[d, q],
            device_id=(row + (-1 if d == 0 else 1), me),
        )

    for c in range(CHUNKS):
        for d in range(4):
            @pl.when(there[d])
            def _():
                send(me, c, d, True).start()
    load.wait()
    for d in range(2):
        @pl.when(halo_there[d])
        def _():
            halo(me, d).start()

    @pl.when(row == 0)
    def _():
        for q in range(count):
            strip[q, 0:HALO, :] = jnp.zeros((HALO, patch_cols), jnp.float32)

    @pl.when(row == ccd_count - 1)
    def _():
        for q in range(count):
            strip[q, rows + HALO : rows + 2 * HALO, :] = jnp.zeros((HALO, patch_cols), jnp.float32)

    def clear(r, carry):
        out[pl.ds(pl.multiple_of(r * HALO, HALO), HALO), :] = jnp.zeros((HALO, cols), jnp.float32)
        return carry

    lax.fori_loop(0, rows // HALO, clear, 0)

    def add_model(q):
        first = pl.multiple_of(q * patch_cols, EDGE)
        wide = patch_cols + 2 * EDGE
        left = pl.multiple_of(jnp.maximum(first - EDGE, 0), EDGE)
        right = pl.multiple_of(jnp.minimum(first + patch_cols, cols - EDGE), EDGE)

        def band(r, carry):
            at = pl.multiple_of(r * BAND, BAND)
            lines = pl.ds(at, BAND)
            pixel = strip[q, pl.ds(at, BAND + 2 * HALO), :].astype(jnp.bfloat16)
            tall = jnp.dot(down[...], pixel, preferred_element_type=jnp.float32)
            tall = tall.astype(jnp.bfloat16)
            v = (
                lax.broadcasted_iota(jnp.int32, (BAND, wide), 0) + r * BAND
            ).astype(jnp.float32) * (2.0 / rows) - (rows - 1) / rows
            model = None
            for b in range(3):
                flat = jnp.dot(
                    tall[b * BAND : (b + 1) * BAND], across[b], preferred_element_type=jnp.float32
                )
                const = weights[b : b + 1, pl.ds(first, wide)]
                slope = weights[3 + b : 4 + b, pl.ds(first, wide)]
                term = (const + slope * v) * flat
                model = term if model is None else model + term
            out[lines, pl.ds(first, patch_cols)] += model[:, EDGE : EDGE + patch_cols]
            out[lines, pl.ds(left, EDGE)] += model[:, :EDGE]
            out[lines, pl.ds(right, EDGE)] += model[:, EDGE + patch_cols :]
            return carry

        lax.fori_loop(0, rows // BAND, band, 0)

    def halos_in(q):
        for d in range(2):
            @pl.when(halo_there[1 - d])
            def _():
                halo(q, d).wait_recv()

    for b in range(3):
        down[b * BAND : (b + 1) * BAND, :] = banded(b, BAND, BAND + 2 * HALO, HALO)

        def fill(i, carry):
            first = pl.multiple_of(i * HALO, HALO)
            across[b, pl.ds(first, HALO), :] = banded(
                b, HALO, patch_cols + 2 * EDGE, EDGE, i * HALO
            )
            return carry

        lax.fori_loop(0, patch_cols // HALO, fill, 0)

    halos_in(me)
    add_model(me)

    def paths(q, c):
        qz, qx = q // inner, q % inner
        along = qx == x
        return (
            along & (qz >= z) & there[0],
            along & (qz <= z) & there[1],
            (qx >= x) & there[2],
            (qx <= x) & there[3],
        )

    table = arrival_codes(count)
    words = []
    for w in range(len(table[0])):
        word = jnp.int32(0)
        for i in range(count):
            word = jnp.where(me == i, jnp.int32(table[i][w]), word)
        words.append(word)

    def arrive(_, words):
        words = list(words)
        digit = words[0] % DIGIT
        for w in range(len(words)):
            words[w] = words[w] // DIGIT
            if w + 1 < len(words):
                words[w] = words[w] + (words[w + 1] % DIGIT) * DIGIT ** (PER_WORD - 1)
        done, event = digit % 2, digit // 2
        q, c = event // CHUNKS, event % CHUNKS
        send(q, c, 0, False).wait_recv()
        onward = paths(q, c)
        for d in range(4):
            @pl.when(onward[d])
            def _():
                send(q, c, d, False).start()
        for d in range(2):
            @pl.when((c == (0 if d == 0 else CHUNKS - 1)) & halo_there[d])
            def _():
                halo(q, d).start()

        @pl.when(done == 1)
        def _():
            halos_in(q)
            add_model(q)

        return tuple(words)

    lax.fori_loop(0, (count - 1) * CHUNKS, arrive, tuple(words))

    def drain(event, carry):
        q, c = event // CHUNKS, event % CHUNKS
        onward = paths(q, c)
        for d in range(4):
            @pl.when(onward[d])
            def _():
                send(q, c, d, False).wait_send()
        for d in range(2):
            @pl.when((c == 0) & halo_there[d])
            def _():
                halo(q, d).wait_send()
        return carry

    lax.fori_loop(0, count * CHUNKS, drain, 0)


def difference_kernel(offsets, exposure, mats, model, weights, out, pixels):
    blocks, depth, block = mats.shape
    pixels[...] = exposure[...].astype(jnp.bfloat16)
    for j in range(blocks):
        start = pl.multiple_of(offsets[j] * block, block)
        value = jnp.dot(
            pixels[:, pl.ds(start, depth)], mats[j], preferred_element_type=jnp.float32
        )
        here = slice(j * block, (j + 1) * block)
        covered = weights[6:7, EDGE + j * block : EDGE + (j + 1) * block]
        out[:, here] = value * covered - model[:, here]


def on_device(exposures, interp, col_offsets, template, coef_table, coef_index, intersection):
    rows, cols = exposures.shape[1:]
    patch_cols = template.shape[1]
    count, ccd_count = lax.axis_size("tile"), lax.axis_size("ccd")
    patch_row = lax.axis_index("ccd")
    my_epoch = lax.axis_index("tile")
    gains = smoothing_gains()

    set_ids = coef_index[my_epoch, patch_row]
    set_pick = (set_ids[:, None] == jnp.arange(KSETS)[None, :]).astype(jnp.float32)
    coef = jnp.sum(set_pick[:, :, None, None] * coef_table[my_epoch][None], axis=1)
    covered = intersection[my_epoch, patch_row].astype(jnp.float32)
    coef = coef * covered[:, None, None] * jnp.asarray(gains, jnp.float32)[None, :, None]
    u = (jnp.arange(patch_cols).astype(jnp.float32) - (patch_cols - 1) / 2.0) / (patch_cols / 2.0)
    spread = coef.transpose(1, 2, 0)[:, :, :, None]
    const = (spread[:, 0] + spread[:, 1] * u[None, None, :]).reshape(3, cols)
    slope = jnp.broadcast_to(spread[:, 2], (3, count, patch_cols)).reshape(3, cols)
    cover = jnp.broadcast_to(covered[None, :, None], (2, count, patch_cols)).reshape(2, cols)
    weights = jnp.pad(jnp.concatenate([const, slope, cover]), ((0, 0), (EDGE, EDGE)))

    in_hbm = pl.BlockSpec(memory_space=pltpu.HBM)
    vmem = pl.BlockSpec(memory_space=pltpu.VMEM)
    model = pl.pallas_call(
        functools.partial(model_kernel, count, ccd_count),
        out_shape=jax.ShapeDtypeStruct((rows, cols), jnp.float32),
        in_specs=[in_hbm, vmem],
        out_specs=vmem,
        scratch_shapes=[
            pltpu.VMEM((count, rows + 2 * HALO, patch_cols), jnp.float32),
            pltpu.VMEM((3 * BAND, BAND + 2 * HALO), jnp.bfloat16),
            pltpu.VMEM((3, patch_cols, patch_cols + 2 * EDGE), jnp.bfloat16),
            pltpu.SemaphoreType.DMA,
            pltpu.SemaphoreType.DMA((4, count, CHUNKS)),
            pltpu.SemaphoreType.DMA((count, CHUNKS)),
            pltpu.SemaphoreType.DMA((2, count)),
            pltpu.SemaphoreType.DMA((2, count)),
        ],
        compiler_params=pltpu.CompilerParams(
            collective_id=0, has_side_effects=True, vmem_limit_bytes=32 * 2**20
        ),
    )(template, weights)

    blocks, depth, block = interp.shape[1:]
    lines = min(LINES, rows)
    result = pl.pallas_call(
        difference_kernel,
        grid=(rows // lines,),
        out_shape=jax.ShapeDtypeStruct((rows, cols), jnp.float32),
        in_specs=[
            pl.BlockSpec(memory_space=pltpu.SMEM),
            pl.BlockSpec((lines, cols), lambda i: (i, 0)),
            pl.BlockSpec((blocks, depth, block), lambda i: (0, 0, 0)),
            pl.BlockSpec((lines, cols), lambda i: (i, 0)),
            pl.BlockSpec(weights.shape, lambda i: (0, 0)),
        ],
        out_specs=pl.BlockSpec((lines, cols), lambda i: (i, 0)),
        scratch_shapes=[pltpu.VMEM((lines, cols), jnp.bfloat16)],
        compiler_params=pltpu.CompilerParams(vmem_limit_bytes=32 * 2**20),
    )(col_offsets[0], exposures[0], interp[0], model, weights)
    return result[None]


def solution(mesh):
    placed = (
        P("tile", "ccd", None),
        P("tile", None, None, None),
        P("tile", None),
        P("ccd", "tile"),
        P(),
        P(),
        P(),
    )
    return jax.shard_map(
        on_device, mesh=mesh, in_specs=placed, out_specs=P("tile", "ccd", None), check_vma=False
    )
```

```python
import functools

import jax
import jax.numpy as jnp
import ml_dtypes
import numpy as np
from jax import lax
from jax.experimental import pallas as pl
from jax.experimental.pallas import tpu as pltpu
from jax.sharding import PartitionSpec as P

HALF = 10
KSETS = 4
SIGMAS = (1.5, 3.0, 5.0)
HALO = 16
EDGE = 128
BAND = 128
CHUNKS = 4
LINES = 128


def basis_taps():
    positions = np.arange(-HALF, HALF + 1).astype(np.float64)
    kernels = []
    for sigma_value in SIGMAS:
        gauss = np.exp(-0.5 * (positions / sigma_value) ** 2)
        kernels.append(gauss / np.sum(gauss))
    return kernels


def smoothing_gains():
    near = [taps.astype(ml_dtypes.bfloat16).astype(np.float64) for taps in basis_taps()]
    return [1.0 / np.sum(taps) ** 2 for taps in near]


def banded(b, rows, cols, shift, first=0):
    shape = (rows, cols)
    distance = (
        lax.broadcasted_iota(jnp.int32, shape, 1)
        - lax.broadcasted_iota(jnp.int32, shape, 0)
        - (shift + first)
    )
    away = distance.astype(jnp.float32)
    taps = jnp.exp(away * away * (-0.5 / SIGMAS[b] ** 2)) * basis_taps()[b][HALF]
    return jnp.where(jnp.abs(away) <= HALF, taps, 0.0).astype(jnp.bfloat16)


def inner_size(count):
    best = 1
    for size in range(1, count + 1):
        if count % size == 0 and size * size <= count:
            best = size
    return best


def arrival_events(count):
    inner = inner_size(count)
    events = []
    for me in range(count):
        z, x = divmod(me, inner)
        near = sorted(range(count // inner), key=lambda other: (abs(other - z), other))
        keys = []
        for q in range(count):
            if q == me:
                continue
            qz, qx = divmod(q, inner)
            away = abs(qz - z)
            time = away if qx == x else max(near.index(qz), away) + abs(qx - x)
            keys.append((time, qx != x, q))
        events.append([q * CHUNKS + c for _, _, q in sorted(keys) for c in range(CHUNKS)])
    return events


DIGIT = 256
PER_WORD = 3


def arrival_codes(count):
    codes = []
    for events in arrival_events(count):
        assert len(events) == (count - 1) * CHUNKS
        left = {q: CHUNKS for q in range(count)}
        digits = []
        for event in events:
            left[event // CHUNKS] -= 1
            digits.append(event * 2 + (left[event // CHUNKS] == 0))
        codes.append([
            sum(int(v) * DIGIT**i for i, v in enumerate(digits[first : first + PER_WORD]))
            for first in range(0, len(digits), PER_WORD)
        ])
    return codes


def model_kernel(
    count, ccd_count, template, weights, out,
    strip, down, across, load_sem, send_sem, recv_sem, hsend_sem, hrecv_sem,
):
    me = lax.axis_index("tile")
    row = lax.axis_index("ccd")
    inner = inner_size(count)
    outer = count // inner
    z, x = me // inner, me % inner
    rows, patch_cols = template.shape
    cols = out.shape[1]
    part = rows // CHUNKS

    targets = (me - inner, me + inner, me - 1, me + 1)
    there = (z > 0, z < outer - 1, x > 0, x < inner - 1)
    halo_there = (row > 0, row < ccd_count - 1)

    load = pltpu.make_async_copy(template, strip.at[me, pl.ds(HALO, rows)], load_sem)
    load.start()

    barrier = pltpu.get_barrier_semaphore()
    total = jnp.int32(0)
    for target, exists in zip(targets, there):
        @pl.when(exists)
        def _():
            pl.semaphore_signal(barrier, inc=1, device_id=(row, target))
        total = total + exists.astype(jnp.int32)
    for step, exists in zip((-1, 1), halo_there):
        @pl.when(exists)
        def _():
            pl.semaphore_signal(barrier, inc=1, device_id=(row + step, me))
        total = total + exists.astype(jnp.int32)
    pl.semaphore_wait(barrier, total)

    def send(q, c, d, own):
        piece = pl.ds(pl.multiple_of(HALO + c * part, HALO), part)
        return pltpu.make_async_remote_copy(
            src_ref=template.at[pl.ds(c * part, part)] if own else strip.at[q, piece],
            dst_ref=strip.at[q, piece],
            send_sem=send_sem.at[d, q, c],
            recv_sem=recv_sem.at[q, c],
            device_id=(row, targets[d]),
        )

    def halo(q, d):
        source = pl.ds(HALO, HALO) if d == 0 else pl.ds(rows, HALO)
        target = pl.ds(HALO + rows, HALO) if d == 0 else pl.ds(0, HALO)
        return pltpu.make_async_remote_copy(
            src_ref=strip.at[q, source],
            dst_ref=strip.at[q, target],
            send_sem=hsend_sem.at[d, q],
            recv_sem=hrecv_sem.at[d, q],
            device_id=(row + (-1 if d == 0 else 1), me),
        )

    for c in range(CHUNKS):
        for d in range(4):
            @pl.when(there[d])
            def _():
                send(me, c, d, True).start()
    load.wait()
    for d in range(2):
        @pl.when(halo_there[d])
        def _():
            halo(me, d).start()

    @pl.when(row == 0)
    def _():
        for q in range(count):
            strip[q, 0:HALO, :] = jnp.zeros((HALO, patch_cols), jnp.float32)

    @pl.when(row == ccd_count - 1)
    def _():
        for q in range(count):
            strip[q, rows + HALO : rows + 2 * HALO, :] = jnp.zeros((HALO, patch_cols), jnp.float32)

    def clear(r, carry):
        out[pl.ds(pl.multiple_of(r * HALO, HALO), HALO), :] = jnp.zeros((HALO, cols), jnp.float32)
        return carry

    lax.fori_loop(0, rows // HALO, clear, 0)

    def add_model(q):
        first = pl.multiple_of(q * patch_cols, EDGE)
        wide = patch_cols + 2 * EDGE
        left = pl.multiple_of(jnp.maximum(first - EDGE, 0), EDGE)
        right = pl.multiple_of(jnp.minimum(first + patch_cols, cols - EDGE), EDGE)

        def band(r, carry):
            at = pl.multiple_of(r * BAND, BAND)
            lines = pl.ds(at, BAND)
            pixel = strip[q, pl.ds(at, BAND + 2 * HALO), :].astype(jnp.bfloat16)
            tall = jnp.dot(down[...], pixel, preferred_element_type=jnp.float32)
            tall = tall.astype(jnp.bfloat16)
            v = (
                lax.broadcasted_iota(jnp.int32, (BAND, wide), 0) + r * BAND
            ).astype(jnp.float32) * (2.0 / rows) - (rows - 1) / rows
            model = None
            for b in range(3):
                flat = jnp.dot(
                    tall[b * BAND : (b + 1) * BAND], across[b], preferred_element_type=jnp.float32
                )
                const = weights[b : b + 1, pl.ds(first, wide)]
                slope = weights[3 + b : 4 + b, pl.ds(first, wide)]
                term = (const + slope * v) * flat
                model = term if model is None else model + term
            out[lines, pl.ds(first, patch_cols)] += model[:, EDGE : EDGE + patch_cols]
            out[lines, pl.ds(left, EDGE)] += model[:, :EDGE]
            out[lines, pl.ds(right, EDGE)] += model[:, EDGE + patch_cols :]
            return carry

        lax.fori_loop(0, rows // BAND, band, 0)

    def halos_in(q):
        for d in range(2):
            @pl.when(halo_there[1 - d])
            def _():
                halo(q, d).wait_recv()

    for b in range(3):
        down[b * BAND : (b + 1) * BAND, :] = banded(b, BAND, BAND + 2 * HALO, HALO)

        def fill(i, carry):
            first = pl.multiple_of(i * HALO, HALO)
            across[b, pl.ds(first, HALO), :] = banded(
                b, HALO, patch_cols + 2 * EDGE, EDGE, i * HALO
            )
            return carry

        lax.fori_loop(0, patch_cols // HALO, fill, 0)

    halos_in(me)
    add_model(me)

    def paths(q, c):
        qz, qx = q // inner, q % inner
        along = qx == x
        return (
            along & (qz >= z) & there[0],
            along & (qz <= z) & there[1],
            (qx >= x) & there[2],
            (qx <= x) & there[3],
        )

    table = arrival_codes(count)
    words = []
    for w in range(len(table[0])):
        word = jnp.int32(0)
        for i in range(count):
            word = jnp.where(me == i, jnp.int32(table[i][w]), word)
        words.append(word)

    def arrive(_, words):
        words = list(words)
        digit = words[0] % DIGIT
        for w in range(len(words)):
            words[w] = words[w] // DIGIT
            if w + 1 < len(words):
                words[w] = words[w] + (words[w + 1] % DIGIT) * DIGIT ** (PER_WORD - 1)
        done, event = digit % 2, digit // 2
        q, c = event // CHUNKS, event % CHUNKS
        send(q, c, 0, False).wait_recv()
        onward = paths(q, c)
        for d in range(4):
            @pl.when(onward[d])
            def _():
                send(q, c, d, False).start()
        for d in range(2):
            @pl.when((c == (0 if d == 0 else CHUNKS - 1)) & halo_there[d])
            def _():
                halo(q, d).start()

        @pl.when(done == 1)
        def _():
            halos_in(q)
            add_model(q)

        return tuple(words)

    lax.fori_loop(0, (count - 1) * CHUNKS, arrive, tuple(words))

    def drain(event, carry):
        q, c = event // CHUNKS, event % CHUNKS
        onward = paths(q, c)
        for d in range(4):
            @pl.when(onward[d])
            def _():
                send(q, c, d, False).wait_send()
        for d in range(2):
            @pl.when((c == 0) & halo_there[d])
            def _():
                halo(q, d).wait_send()
        return carry

    lax.fori_loop(0, count * CHUNKS, drain, 0)


def difference_kernel(offsets, exposure, mats, model, weights, out, pixels):
    blocks, depth, block = mats.shape
    pixels[...] = exposure[...].astype(jnp.bfloat16)
    for j in range(blocks):
        start = pl.multiple_of(offsets[j] * block, block)
        value = jnp.dot(
            pixels[:, pl.ds(start, depth)], mats[j], preferred_element_type=jnp.float32
        )
        here = slice(j * block, (j + 1) * block)
        covered = weights[6:7, EDGE + j * block : EDGE + (j + 1) * block]
        out[:, here] = value * covered - model[:, here]


def on_device(exposures, interp, col_offsets, template, coef_table, coef_index, intersection):
    rows, cols = exposures.shape[1:]
    patch_cols = template.shape[1]
    count, ccd_count = lax.axis_size("tile"), lax.axis_size("ccd")
    patch_row = lax.axis_index("ccd")
    my_epoch = lax.axis_index("tile")
    gains = smoothing_gains()

    set_ids = coef_index[my_epoch, patch_row]
    set_pick = (set_ids[:, None] == jnp.arange(KSETS)[None, :]).astype(jnp.float32)
    coef = jnp.sum(set_pick[:, :, None, None] * coef_table[my_epoch][None], axis=1)
    covered = intersection[my_epoch, patch_row].astype(jnp.float32)
    coef = coef * covered[:, None, None] * jnp.asarray(gains, jnp.float32)[None, :, None]
    u = (jnp.arange(patch_cols).astype(jnp.float32) - (patch_cols - 1) / 2.0) / (patch_cols / 2.0)
    spread = coef.transpose(1, 2, 0)[:, :, :, None]
    const = (spread[:, 0] + spread[:, 1] * u[None, None, :]).reshape(3, cols)
    slope = jnp.broadcast_to(spread[:, 2], (3, count, patch_cols)).reshape(3, cols)
    cover = jnp.broadcast_to(covered[None, :, None], (2, count, patch_cols)).reshape(2, cols)
    weights = jnp.pad(jnp.concatenate([const, slope, cover]), ((0, 0), (EDGE, EDGE)))

    in_hbm = pl.BlockSpec(memory_space=pltpu.HBM)
    vmem = pl.BlockSpec(memory_space=pltpu.VMEM)
    model = pl.pallas_call(
        functools.partial(model_kernel, count, ccd_count),
        out_shape=jax.ShapeDtypeStruct((rows, cols), jnp.float32),
        in_specs=[in_hbm, vmem],
        out_specs=vmem,
        scratch_shapes=[
            pltpu.VMEM((count, rows + 2 * HALO, patch_cols), jnp.float32),
            pltpu.VMEM((3 * BAND, BAND + 2 * HALO), jnp.bfloat16),
            pltpu.VMEM((3, patch_cols, patch_cols + 2 * EDGE), jnp.bfloat16),
            pltpu.SemaphoreType.DMA,
            pltpu.SemaphoreType.DMA((4, count, CHUNKS)),
            pltpu.SemaphoreType.DMA((count, CHUNKS)),
            pltpu.SemaphoreType.DMA((2, count)),
            pltpu.SemaphoreType.DMA((2, count)),
        ],
        compiler_params=pltpu.CompilerParams(
            collective_id=0, has_side_effects=True, vmem_limit_bytes=32 * 2**20
        ),
    )(template, weights)

    blocks, depth, block = interp.shape[1:]
    lines = min(LINES, rows)
    result = pl.pallas_call(
        difference_kernel,
        grid=(rows // lines,),
        out_shape=jax.ShapeDtypeStruct((rows, cols), jnp.float32),
        in_specs=[
            pl.BlockSpec(memory_space=pltpu.SMEM),
            pl.BlockSpec((lines, cols), lambda i: (i, 0)),
            pl.BlockSpec((blocks, depth, block), lambda i: (0, 0, 0)),
            pl.BlockSpec((lines, cols), lambda i: (i, 0)),
            pl.BlockSpec(weights.shape, lambda i: (0, 0)),
        ],
        out_specs=pl.BlockSpec((lines, cols), lambda i: (i, 0)),
        scratch_shapes=[pltpu.VMEM((lines, cols), jnp.bfloat16)],
        compiler_params=pltpu.CompilerParams(vmem_limit_bytes=32 * 2**20),
    )(col_offsets[0], exposures[0], interp[0], model, weights)
    return result[None]


def solution(mesh):
    placed = (
        P("tile", "ccd", None),
        P("tile", None, None, None),
        P("tile", None),
        P("ccd", "tile"),
        P(),
        P(),
        P(),
    )
    return jax.shard_map(
        on_device, mesh=mesh, in_specs=placed, out_specs=P("tile", "ccd", None), check_vma=False
    )
```
